32 devices in a mesh: groups: 2 (over y), seq: 4 (over z), col: 4 (over x, core).
Axes of the slice: x: 2, y: 2, z: 4, core: 2. Of those that a mesh axis runs over, the one named last changes fastest.
Arguments:
- embeddings: bfloat16 [8192, 1280], P(('groups', 'seq'), 'col'), parts along dimension 0, may hold values from -12 to 12
- residues: int32 [8192, 1024], P(('groups', 'seq'), 'col'), parts along dimension 0, may hold values from 0 to 20
Outputs:
- sequence_weight_vector: float32 [8192], P(('groups', 'seq')), parts along dimension 0
- profile: float32 [21, 2048], P(None, ('groups', 'col')), parts along dimension 1
The draws below stay inside these ranges and needn't reach their ends.
There are 2 independent parts, one for each index of `groups`. The reference program is written for one: setup_inputs(seed, part) draws one part's arguments, and reference() takes and returns one part's arrays. A program takes and returns all parts, laid end to end along the dimension named above; each array names one. Nothing has to cross between parts.
All inputs are finite; a program needn't handle non-finite values.
Results may differ from the reference program's by a relative error of at most 0.0003.
Values may be sent and summed in bfloat16 or wider, within the bound.
A program may use at most 64 MiB of HBM per device.

```python
import math
import jax
import jax.numpy as jnp
from jax import lax

FEATURE_LENGTH = 1280
L = 1024
SYMBOLS = 21
S_DEV = 1024
BLOCKS = 4
SEQS = 4096
ROUNDS = 1
STRIDE = 1


def draw_embeddings(key, part):
    key = jax.random.fold_in(key, 11)
    noise_key, axis_key, scale_key = jax.random.split(key, 3)
    jitter = jnp.clip(jax.random.normal(noise_key, (SEQS, FEATURE_LENGTH), jnp.float32), -4.0, 4.0)
    spread = jnp.exp(jax.random.uniform(scale_key, (SEQS,), jnp.float32, math.log(0.15), math.log(1.2)))
    direction = jnp.clip(jax.random.normal(axis_key, (FEATURE_LENGTH,), jnp.float32), -4.0, 4.0)
    position = (jnp.arange(SEQS) // S_DEV).astype(jnp.float32) / max(BLOCKS - 1, 1)
    lifted = spread * (0.4 + 0.9 * position)
    return (jitter + lifted[:, None] * direction[None, :]).astype(jnp.bfloat16)


def draw_residues(key, part):
    key = jax.random.fold_in(key, 23)
    base_key, one_key, two_key, keep_key = jax.random.split(key, 4)
    column_base = jax.random.randint(base_key, (L,), 0, SYMBOLS)
    draw_one = jax.random.randint(one_key, (SEQS, L), 0, SYMBOLS)
    draw_two = jax.random.randint(two_key, (SEQS, L), 0, SYMBOLS)
    conserved = jax.random.randint(keep_key, (L,), 0, 2)
    moved = jnp.where(conserved[None, :] == 1, jnp.minimum(draw_one, draw_two), draw_one)
    return ((column_base[None, :] + moved) % SYMBOLS).astype(jnp.int32)


def setup_inputs(seed: int = 0, part: int = 0) -> dict:
    seeds = jax.random.split(jax.random.key(seed), 3)
    own_keys = jax.random.split(jax.random.fold_in(seeds[2], part), 3)
    embeddings = draw_embeddings(jax.random.fold_in(jax.random.fold_in(seeds[2], part), 71), part)
    residues = draw_residues(jax.random.fold_in(jax.random.fold_in(seeds[2], part), 71), part)
    return {"embeddings": embeddings, "residues": residues}


similarity_limit = 0.5
sigmoid_sharpness_scale = 0.05


def reference(embeddings, residues):
    blocks = embeddings.reshape(BLOCKS, S_DEV, FEATURE_LENGTH)
    start_positions = [0]
    for round_index in range(ROUNDS):
        distance = 1 + round_index * STRIDE
        start_positions.append(distance)
        start_positions.append(-distance)

    def block_counts(index_of_block):
        left_rows = blocks[index_of_block]
        nearby_counts_summed = jnp.zeros((S_DEV,), jnp.float32)
        for offset in start_positions:
            neighbour = blocks[(index_of_block + offset + BLOCKS) % BLOCKS]
            pairwise_agreement = jnp.dot(left_rows, neighbour.T, preferred_element_type=jnp.float32)
            nearby_counts_summed = nearby_counts_summed + jnp.sum(jax.nn.sigmoid((pairwise_agreement / FEATURE_LENGTH - similarity_limit) / sigmoid_sharpness_scale), axis=1)
        return nearby_counts_summed

    counts = lax.map(block_counts, jnp.arange(BLOCKS, dtype=jnp.int32)).reshape(SEQS)
    weights = 1.0 / counts
    weight_sum = jnp.sum(weights)
    summed = jnp.stack([jnp.sum(jnp.where(residues == symbol, weights[:, None], jnp.zeros((), jnp.float32)), axis=0) for symbol in range(SYMBOLS)])
    return weights * (SEQS / weight_sum), summed / weight_sum
```

```python
import functools
import math

import jax
import jax.numpy as jnp
from jax import lax
from jax.experimental import pallas as pl
from jax.experimental.pallas import tpu as pltpu
from jax.sharding import PartitionSpec as P

SYMBOLS = 21
TABLE_ROWS = 24
COLS = 4

similarity_limit = 0.5
sigmoid_sharpness_scale = 0.05


def round_distances(block_count):
    round_count = min(4, (block_count - 1) // 2)
    stride = max(1, block_count // 8)
    return [1 + r * stride for r in range(round_count)]


def butterfly_sum(terms):
    while len(terms) > 1:
        half = len(terms) // 2
        terms = [terms[i] + terms[i + half] for i in range(half)]
    return terms[0]


def sigmoid_of(products, feature_length):
    log2e = math.log2(math.e)
    slope = -log2e / (feature_length * sigmoid_sharpness_scale)
    shift = log2e * similarity_limit / sigmoid_sharpness_scale
    return 1.0 / (1.0 + jnp.exp2(jnp.minimum(products * slope + shift, 126.0)))


def kernel(
    n, distances, quarter,
    x_ref, res_ref, weight_ref, profile_ref,
    gathered, zone, own, partner, onehot, rows_out, rows_in, back_out, back_in, table_out, table_in,
    xs, xr, ss, sr, fs, fr, zs, zr, cs, cr, ks, kr, ps, pr,
):
    width = x_ref.shape[1]
    feature_length = width * COLS
    half = quarter // 2
    me = lax.axis_index("col")
    block = lax.axis_index("seq")
    group = lax.axis_index("groups")
    cols = [me, me + 1 - 2 * (me % 2), (me + 2) % 4, 3 - me]

    def device(o, k):
        return (group, lax.rem(block + (o % n), n), cols[k])

    peers = {(0, k) for k in range(1, COLS)}
    peers |= {(s * d % n, k) for d in distances for s in (1, -1) for k in range(COLS)}
    peers |= {(o, 0) for o in range(1, n)}
    peers = sorted(peers)

    barrier = pltpu.get_barrier_semaphore()
    for o, k in peers:
        pl.semaphore_signal(
            barrier, inc=1, device_id=device(o, k), device_id_type=pl.DeviceIdType.MESH
        )
    for r in range(COLS):
        start = pl.multiple_of(cols[r] * quarter, quarter)
        rows = x_ref[pl.ds(start, quarter), :]
        gathered[0, r, 0:quarter, :] = rows[:, 0:128]
        gathered[0, r, quarter : 2 * quarter, :] = rows[:, 128:256]
        gathered[0, r, 2 * quarter : 2 * quarter + half, :] = jnp.concatenate(
            [rows[:half, 256:320], rows[half:, 256:320]], axis=1
        )
    pl.semaphore_wait(barrier, len(peers))

    started = []

    def send(src, dst, send_sem, recv_sem, o, k):
        copy = pltpu.make_async_remote_copy(
            src_ref=src, dst_ref=dst, send_sem=send_sem, recv_sem=recv_sem,
            device_id=device(o, k), device_id_type=pl.DeviceIdType.MESH,
        )
        copy.start()
        started.append(copy)

    def arrived(dst, recv_sem):
        pltpu.make_async_copy(dst, dst, recv_sem).wait()

    def send_on_z(slot):
        for i, d in enumerate(distances):
            send(gathered.at[slot, 0], zone.at[i, slot], zs.at[i, slot], zr.at[i, slot], d, 0)

    def pass_to_sibling(r):
        arrived(gathered.at[2, r], xr.at[r])
        send(gathered.at[2, r], gathered.at[3, r ^ 1], fs.at[r], fr.at[r ^ 1], 0, 1)

    for r in (3, 2, 0, 1):
        send(gathered.at[0, r], gathered.at[2, r ^ 2], xs.at[r], xr.at[r ^ 2], 0, 2)
    send_on_z(0)
    for r in (1, 0, 3, 2):
        send(gathered.at[0, r], gathered.at[1, r ^ 1], ss.at[r], sr.at[r ^ 1], 0, 1)
    arrived(gathered.at[1, 0], sr.at[0])
    send_on_z(1)

    def spread(r):
        start = pl.multiple_of(cols[r] * quarter, quarter)
        codes = res_ref[pl.ds(start, quarter), :]
        for symbol in range(SYMBOLS):
            onehot[symbol, r * quarter : (r + 1) * quarter, :] = jnp.where(
                codes == symbol, 1.0, 0.0
            ).astype(jnp.bfloat16)

    def assemble(parts, target, first):
        for slot in range(COLS):
            part = parts(slot)
            target[first : first + quarter, slot * 256 : slot * 256 + 128] = part[0:quarter, :]
            target[first : first + quarter, slot * 256 + 128 : slot * 256 + 256] = part[
                quarter : 2 * quarter, :
            ]
        for pair in range(COLS // 2):
            one = parts(2 * pair)[2 * quarter : 2 * quarter + half, :]
            two = parts(2 * pair + 1)[2 * quarter : 2 * quarter + half, :]
            at = COLS * 256 + pair * 128
            target[first : first + half, at : at + 128] = jnp.concatenate(
                [one[:, :64], two[:, :64]], axis=1
            )
            target[first + half : first + quarter, at : at + 128] = jnp.concatenate(
                [one[:, 64:], two[:, 64:]], axis=1
            )

    def agreement(left, r):
        products = lax.dot_general(
            left, own[r * quarter : (r + 1) * quarter, :],
            (((1,), (1,)), ((), ())), preferred_element_type=jnp.float32,
        )
        return sigmoid_of(products, feature_length)

    spread(0)
    pass_to_sibling(1)
    pass_to_sibling(0)
    send_on_z(2)
    arrived(gathered.at[3, 0], fr.at[0])
    send_on_z(3)
    sums = []
    for r in range(COLS):
        if r > 0:
            spread(r)
        if r > 1:
            pass_to_sibling(r)
        if r == 1 or r == 3:
            for q in (r - 1, r):
                if q > 0:
                    arrived(gathered.at[1, q], sr.at[q])
                    arrived(gathered.at[3, q], fr.at[q])
                assemble(lambda slot: gathered[slot, q], own, q * quarter)
                sums.append(
                    jnp.sum(agreement(own[0:quarter, :], q), axis=0, keepdims=True)
                )

    for i, d in enumerate(distances):
        for slot in range(COLS):
            arrived(zone.at[i, slot], zr.at[i, slot])
        assemble(lambda slot: zone[i, slot], partner, 0)
        across = jnp.zeros((quarter, 128), jnp.float32)
        for r in range(COLS):
            values = agreement(partner[...], r)
            sums[r] = sums[r] + jnp.sum(values, axis=0, keepdims=True)
            for lane in range(0, quarter, 128):
                across = across + values[:, lane : lane + 128]
        back = jnp.sum(across.T, axis=0, keepdims=True)
        back_out[i] = jnp.broadcast_to(back, (8, quarter))
        for k in range(COLS):
            send(back_out.at[i], back_in.at[i, k], ks.at[i, k], kr.at[i, k], -d, k)
    for r in range(COLS):
        rows_out[r : r + 1, :] = sums[r]
        rows_out[r + COLS : r + COLS + 1, :] = sums[r]
    for k in range(1, COLS):
        send(rows_out, rows_in.at[k], cs.at[k], cr.at[k], 0, k)
    for k in range(1, COLS):
        arrived(rows_in.at[k], cr.at[k])
    for i in range(len(distances)):
        for k in range(COLS):
            arrived(back_in.at[i, k], kr.at[i, k])

    weights = []
    for r in range(COLS):
        terms = [sums[r]] + [rows_in[k, r ^ k : (r ^ k) + 1, :] for k in range(1, COLS)]
        counts = (terms[0] + terms[1]) + (terms[2] + terms[3])
        for i in range(len(distances)):
            counts = counts + back_in[i, r, 0:1, :]
        weights.append(1.0 / counts)
    local_total = jnp.sum(
        (weights[0] + weights[1]) + (weights[2] + weights[3]), axis=1, keepdims=True
    )

    whole = jnp.concatenate(weights, axis=1)
    high = whole.astype(jnp.bfloat16).astype(jnp.float32)
    rest = whole - high
    middle = rest.astype(jnp.bfloat16).astype(jnp.float32)
    low = rest - middle
    row = lax.broadcasted_iota(jnp.int32, (16, whole.shape[1]), 0)
    split = jnp.where(
        row == 0, high, jnp.where(row == 1, middle, jnp.where(row == 2, low, 0.0))
    ).astype(jnp.bfloat16)
    for symbol in range(SYMBOLS):
        part = jnp.dot(split, onehot[symbol], preferred_element_type=jnp.float32)
        table_out[symbol : symbol + 1, :] = jnp.sum(part, axis=0, keepdims=True)
    table_out[SYMBOLS:TABLE_ROWS, :] = jnp.broadcast_to(
        local_total, (TABLE_ROWS - SYMBOLS, table_out.shape[1])
    )
    for o in range(1, n):
        send(table_out, table_in.at[o], ps.at[o], pr.at[o], o, 0)
    for o in range(1, n):
        arrived(table_in.at[o], pr.at[o])
    table = butterfly_sum([table_out[...]] + [table_in[o] for o in range(1, n)])
    weight_sum = table[SYMBOLS : SYMBOLS + 1, :]
    profile_ref[...] = table[:SYMBOLS, :] / weight_sum
    scale = (n * COLS * quarter) / weight_sum
    for r in range(COLS):
        scaled = weights[r] * scale
        for piece in range(quarter // 128):
            weight_ref[pl.ds(cols[r] * (quarter // 128) + piece, 1), :] = scaled[
                :, piece * 128 : piece * 128 + 128
            ]
    for copy in started:
        copy.wait_send()


def body(n, embeddings, residues):
    rows, width = embeddings.shape
    columns = residues.shape[1]
    quarter = rows // COLS
    distances = round_distances(n)
    nd = len(distances)
    packed = quarter * width // 128
    dma = pltpu.SemaphoreType.DMA
    weights, profile = pl.pallas_call(
        functools.partial(kernel, n, distances, quarter),
        out_shape=(
            jax.ShapeDtypeStruct((rows // 128, 128), jnp.float32),
            jax.ShapeDtypeStruct((SYMBOLS, columns), jnp.float32),
        ),
        in_specs=[pl.BlockSpec(memory_space=pltpu.VMEM)] * 2,
        out_specs=[pl.BlockSpec(memory_space=pltpu.VMEM)] * 2,
        scratch_shapes=[
            pltpu.VMEM((COLS, COLS, packed, 128), jnp.bfloat16),
            pltpu.VMEM((nd, COLS, packed, 128), jnp.bfloat16),
            pltpu.VMEM((rows, width * COLS), jnp.bfloat16),
            pltpu.VMEM((quarter, width * COLS), jnp.bfloat16),
            pltpu.VMEM((SYMBOLS, rows, columns), jnp.bfloat16),
            pltpu.VMEM((8, quarter), jnp.float32),
            pltpu.VMEM((COLS, 8, quarter), jnp.float32),
            pltpu.VMEM((nd, 8, quarter), jnp.float32),
            pltpu.VMEM((nd, COLS, 8, quarter), jnp.float32),
            pltpu.VMEM((TABLE_ROWS, columns), jnp.float32),
            pltpu.VMEM((n, TABLE_ROWS, columns), jnp.float32),
            dma((COLS,)), dma((COLS,)), dma((COLS,)), dma((COLS,)), dma((COLS,)), dma((COLS,)),
            dma((nd, COLS)), dma((nd, COLS)), dma((COLS,)), dma((COLS,)),
            dma((nd, COLS)), dma((nd, COLS)), dma((n,)), dma((n,)),
        ],
        compiler_params=pltpu.CompilerParams(
            collective_id=0, has_side_effects=True, vmem_limit_bytes=48 * 1024 * 1024
        ),
    )(embeddings, residues)
    return weights.reshape(rows), profile


def solution(mesh):
    return jax.shard_map(
        functools.partial(body, mesh.shape["seq"]),
        mesh=mesh,
        in_specs=(P(("groups", "seq"), "col"), P(("groups", "seq"), "col")),
        out_specs=(P(("groups", "seq")), P(None, ("groups", "col"))),
        check_vma=False,
    )
```

```python
import functools
import math

import jax
import jax.numpy as jnp
from jax import lax
from jax.experimental import pallas as pl
from jax.experimental.pallas import tpu as pltpu
from jax.sharding import PartitionSpec as P

SYMBOLS = 21
TABLE_ROWS = 24
COLS = 4

similarity_limit = 0.5
sigmoid_sharpness_scale = 0.05


def round_distances(block_count):
    round_count = min(4, (block_count - 1) // 2)
    stride = max(1, block_count // 8)
    return [1 + r * stride for r in range(round_count)]


def butterfly_sum(terms):
    while len(terms) > 1:
        half = len(terms) // 2
        terms = [terms[i] + terms[i + half] for i in range(half)]
    return terms[0]


def sigmoid_of(products, feature_length):
    log2e = math.log2(math.e)
    slope = -log2e / (feature_length * sigmoid_sharpness_scale)
    shift = log2e * similarity_limit / sigmoid_sharpness_scale
    return 1.0 / (1.0 + jnp.exp2(jnp.minimum(products * slope + shift, 126.0)))


def kernel(
    n, distances, quarter,
    x_ref, res_ref, weight_ref, profile_ref,
    gathered, zone, left, residues, onehot, rows_out, rows_in, back_out, back_in, table_out, table_in,
    ls, rs, xs, xr, ss, sr, fs, fr, zs, zr, cs, cr, ks, kr, ps, pr,
):
    width = x_ref.shape[0]
    feature_length = width * COLS
    me = lax.axis_index("col")
    block = lax.axis_index("seq")
    group = lax.axis_index("groups")
    cols = [me, me + 1 - 2 * (me % 2), (me + 2) % 4, 3 - me]

    def device(o, k):
        return (group, lax.rem(block + (o % n), n), cols[k])

    def piece(slot, r):
        return gathered.at[r, pl.ds(slot * width, width), :]

    peers = {(0, k) for k in range(1, COLS)}
    peers |= {(s * d % n, k) for d in distances for s in (1, -1) for k in range(COLS)}
    peers |= {(o, 0) for o in range(1, n)}
    peers = sorted(peers)

    barrier = pltpu.get_barrier_semaphore()
    for o, k in peers:
        pl.semaphore_signal(
            barrier, inc=1, device_id=device(o, k), device_id_type=pl.DeviceIdType.MESH
        )
    loads = []
    for r in (3, 2, 0, 1):
        start = pl.multiple_of(cols[r] * quarter, quarter)
        loads.append(
            pltpu.make_async_copy(x_ref.at[:, pl.ds(start, quarter)], piece(0, r), ls.at[r])
        )
    fetch_residues = pltpu.make_async_copy(res_ref, residues, rs)
    for load in loads:
        load.start()
    fetch_residues.start()
    for load in loads:
        load.wait()
    pl.semaphore_wait(barrier, len(peers))

    started = []

    def send(src, dst, send_sem, recv_sem, o, k):
        copy = pltpu.make_async_remote_copy(
            src_ref=src, dst_ref=dst, send_sem=send_sem, recv_sem=recv_sem,
            device_id=device(o, k), device_id_type=pl.DeviceIdType.MESH,
        )
        copy.start()
        started.append(copy)

    def arrived(dst, recv_sem):
        pltpu.make_async_copy(dst, dst, recv_sem).wait()

    def send_on_z(slot):
        for i, d in enumerate(distances):
            send(
                piece(slot, 0), zone.at[i, pl.ds(slot * width, width), :],
                zs.at[i, slot], zr.at[i, slot], d, 0,
            )

    def pass_to_sibling(r):
        arrived(piece(2, r), xr.at[r])
        send(piece(2, r), piece(3, r ^ 1), fs.at[r], fr.at[r ^ 1], 0, 1)

    for r in (3, 2, 0, 1):
        send(piece(0, r), piece(2, r ^ 2), xs.at[r], xr.at[r ^ 2], 0, 2)
    send_on_z(0)
    for r in (1, 0, 3, 2):
        send(piece(0, r), piece(1, r ^ 1), ss.at[r], sr.at[r ^ 1], 0, 1)
    arrived(piece(1, 0), sr.at[0])
    send_on_z(1)
    fetch_residues.wait()

    def spread(r):
        start = pl.multiple_of(cols[r] * quarter, quarter)
        codes = residues[pl.ds(start, quarter), :]
        for symbol in range(SYMBOLS):
            onehot[symbol, r * quarter : (r + 1) * quarter, :] = jnp.where(
                codes == symbol, 1.0, 0.0
            ).astype(jnp.bfloat16)

    def agreement(r):
        products = jnp.dot(left[...], gathered[r], preferred_element_type=jnp.float32)
        return sigmoid_of(products, feature_length)

    spread(0)
    pass_to_sibling(1)
    pass_to_sibling(0)
    send_on_z(2)
    arrived(piece(3, 0), fr.at[0])
    send_on_z(3)
    sums = []
    for r in range(COLS):
        if r > 0:
            spread(r)
        if r > 1:
            pass_to_sibling(r)
        if r == 1 or r == 3:
            for q in (r - 1, r):
                if q > 0:
                    arrived(piece(1, q), sr.at[q])
                    arrived(piece(3, q), fr.at[q])
                else:
                    left[...] = gathered[0].T
                sums.append(jnp.sum(agreement(q), axis=0, keepdims=True))

    for i, d in enumerate(distances):
        for slot in range(COLS):
            arrived(zone.at[i, pl.ds(slot * width, width), :], zr.at[i, slot])
        left[...] = zone[i].T
        across = jnp.zeros((quarter, 128), jnp.float32)
        for r in range(COLS):
            values = agreement(r)
            sums[r] = sums[r] + jnp.sum(values, axis=0, keepdims=True)
            for lane in range(0, quarter, 128):
                across = across + values[:, lane : lane + 128]
        back = jnp.sum(across.T, axis=0, keepdims=True)
        back_out[i] = jnp.broadcast_to(back, (8, quarter))
        for k in range(COLS):
            send(back_out.at[i], back_in.at[i, k], ks.at[i, k], kr.at[i, k], -d, k)
    for r in range(COLS):
        rows_out[r : r + 1, :] = sums[r]
        rows_out[r + COLS : r + COLS + 1, :] = sums[r]
    for k in range(1, COLS):
        send(rows_out, rows_in.at[k], cs.at[k], cr.at[k], 0, k)
    for k in range(1, COLS):
        arrived(rows_in.at[k], cr.at[k])
    for i in range(len(distances)):
        for k in range(COLS):
            arrived(back_in.at[i, k], kr.at[i, k])

    weights = []
    for r in range(COLS):
        terms = [sums[r]] + [rows_in[k, r ^ k : (r ^ k) + 1, :] for k in range(1, COLS)]
        counts = (terms[0] + terms[1]) + (terms[2] + terms[3])
        for i in range(len(distances)):
            counts = counts + back_in[i, r, 0:1, :]
        weights.append(1.0 / counts)
    local_total = jnp.sum(
        (weights[0] + weights[1]) + (weights[2] + weights[3]), axis=1, keepdims=True
    )

    whole = jnp.concatenate(weights, axis=1)
    high = whole.astype(jnp.bfloat16).astype(jnp.float32)
    rest = whole - high
    middle = rest.astype(jnp.bfloat16).astype(jnp.float32)
    low = rest - middle
    row = lax.broadcasted_iota(jnp.int32, (16, whole.shape[1]), 0)
    split = jnp.where(
        row == 0, high, jnp.where(row == 1, middle, jnp.where(row == 2, low, 0.0))
    ).astype(jnp.bfloat16)
    for symbol in range(SYMBOLS):
        part = jnp.dot(split, onehot[symbol], preferred_element_type=jnp.float32)
        table_out[symbol : symbol + 1, :] = jnp.sum(part, axis=0, keepdims=True)
    table_out[SYMBOLS:TABLE_ROWS, :] = jnp.broadcast_to(
        local_total, (TABLE_ROWS - SYMBOLS, table_out.shape[1])
    )
    for o in range(1, n):
        send(table_out, table_in.at[o], ps.at[o], pr.at[o], o, 0)
    for o in range(1, n):
        arrived(table_in.at[o], pr.at[o])
    table = butterfly_sum([table_out[...]] + [table_in[o] for o in range(1, n)])
    weight_sum = table[SYMBOLS : SYMBOLS + 1, :]
    profile_ref[...] = table[:SYMBOLS, :] / weight_sum
    scale = (n * COLS * quarter) / weight_sum
    for r in range(COLS):
        scaled = weights[r] * scale
        for part in range(quarter // 128):
            weight_ref[pl.ds(cols[r] * (quarter // 128) + part, 1), :] = scaled[
                :, part * 128 : part * 128 + 128
            ]
    for copy in started:
        copy.wait_send()


def body(n, embeddings, residues):
    rows, width = embeddings.shape
    columns = residues.shape[1]
    quarter = rows // COLS
    distances = round_distances(n)
    nd = len(distances)
    dma = pltpu.SemaphoreType.DMA
    weights, profile = pl.pallas_call(
        functools.partial(kernel, n, distances, quarter),
        out_shape=(
            jax.ShapeDtypeStruct((rows // 128, 128), jnp.float32),
            jax.ShapeDtypeStruct((SYMBOLS, columns), jnp.float32),
        ),
        in_specs=[pl.BlockSpec(memory_space=pltpu.HBM)] * 2,
        out_specs=[pl.BlockSpec(memory_space=pltpu.VMEM)] * 2,
        scratch_shapes=[
            pltpu.VMEM((COLS, width * COLS, quarter), jnp.bfloat16),
            pltpu.VMEM((nd, width * COLS, quarter), jnp.bfloat16),
            pltpu.VMEM((quarter, width * COLS), jnp.bfloat16),
            pltpu.VMEM((rows, columns), jnp.int32),
            pltpu.VMEM((SYMBOLS, rows, columns), jnp.bfloat16),
            pltpu.VMEM((8, quarter), jnp.float32),
            pltpu.VMEM((COLS, 8, quarter), jnp.float32),
            pltpu.VMEM((nd, 8, quarter), jnp.float32),
            pltpu.VMEM((nd, COLS, 8, quarter), jnp.float32),
            pltpu.VMEM((TABLE_ROWS, columns), jnp.float32),
            pltpu.VMEM((n, TABLE_ROWS, columns), jnp.float32),
            dma((COLS,)), dma,
            dma((COLS,)), dma((COLS,)), dma((COLS,)), dma((COLS,)), dma((COLS,)), dma((COLS,)),
            dma((nd, COLS)), dma((nd, COLS)), dma((COLS,)), dma((COLS,)),
            dma((nd, COLS)), dma((nd, COLS)), dma((n,)), dma((n,)),
        ],
        compiler_params=pltpu.CompilerParams(
            collective_id=0, has_side_effects=True, vmem_limit_bytes=48 * 1024 * 1024
        ),
    )(embeddings.T, residues)
    return weights.reshape(rows), profile


def solution(mesh):
    return jax.shard_map(
        functools.partial(body, mesh.shape["seq"]),
        mesh=mesh,
        in_specs=(P(("groups", "seq"), "col"), P(("groups", "seq"), "col")),
        out_specs=(P(("groups", "seq")), P(None, ("groups", "col"))),
        check_vma=False,
    )
```

```python
import functools
import math

import jax
import jax.numpy as jnp
from jax import lax
from jax.experimental import pallas as pl
from jax.experimental.pallas import tpu as pltpu
from jax.sharding import PartitionSpec as P

SYMBOLS = 21
TABLE_ROWS = 24
COLS = 4

similarity_limit = 0.5
sigmoid_sharpness_scale = 0.05


def round_distances(block_count):
    round_count = min(4, (block_count - 1) // 2)
    stride = max(1, block_count // 8)
    return [1 + r * stride for r in range(round_count)]


def butterfly_sum(terms):
    while len(terms) > 1:
        half = len(terms) // 2
        terms = [terms[i] + terms[i + half] for i in range(half)]
    return terms[0]


def sigmoid_of(products, feature_length):
    log2e = math.log2(math.e)
    slope = -log2e / (feature_length * sigmoid_sharpness_scale)
    shift = log2e * similarity_limit / sigmoid_sharpness_scale
    return 1.0 / (1.0 + jnp.exp2(jnp.minimum(products * slope + shift, 126.0)))


def kernel(
    n, distances, quarter,
    x_ref, res_ref, weight_ref, profile_ref,
    gathered, zone, left, residues, onehot, rows_out, rows_in, back_out, back_in, table_out, table_in,
    ls, rs, xs, xr, ss, sr, fs, fr, zs, zr, cs, cr, ks, kr, ps, pr,
):
    width = x_ref.shape[0]
    feature_length = width * COLS
    me = lax.axis_index("col")
    block = lax.axis_index("seq")
    group = lax.axis_index("groups")
    cols = [me, me + 1 - 2 * (me % 2), (me + 2) % 4, 3 - me]

    def device(o, k):
        return (group, lax.rem(block + (o % n), n), cols[k])

    def piece(slot, r):
        return gathered.at[r, pl.ds(slot * width, width), :]

    peers = {(0, k) for k in range(1, COLS)}
    peers |= {(s * d % n, k) for d in distances for s in (1, -1) for k in range(COLS)}
    peers |= {(o, 0) for o in range(1, n)}
    peers = sorted(peers)

    barrier = pltpu.get_barrier_semaphore()
    for o, k in peers:
        pl.semaphore_signal(
            barrier, inc=1, device_id=device(o, k), device_id_type=pl.DeviceIdType.MESH
        )
    loads = []
    for r in (3, 2, 0, 1):
        start = pl.multiple_of(cols[r] * quarter, quarter)
        loads.append(
            pltpu.make_async_copy(x_ref.at[:, pl.ds(start, quarter)], piece(0, r), ls.at[r])
        )
    fetch_residues = pltpu.make_async_copy(res_ref, residues, rs)
    for load in loads:
        load.start()
    fetch_residues.start()
    for load in loads:
        load.wait()
    pl.semaphore_wait(barrier, len(peers))

    started = []

    def send(src, dst, send_sem, recv_sem, o, k):
        copy = pltpu.make_async_remote_copy(
            src_ref=src, dst_ref=dst, send_sem=send_sem, recv_sem=recv_sem,
            device_id=device(o, k), device_id_type=pl.DeviceIdType.MESH,
        )
        copy.start()
        started.append(copy)

    def arrived(dst, recv_sem):
        pltpu.make_async_copy(dst, dst, recv_sem).wait()

    def send_on_z(slot):
        for i, d in enumerate(distances):
            send(
                piece(slot, 0), zone.at[i, pl.ds(slot * width, width), :],
                zs.at[i, slot], zr.at[i, slot], d, 0,
            )

    def pass_to_sibling(r):
        arrived(piece(2, r), xr.at[r])
        send(piece(2, r), piece(3, r ^ 1), fs.at[r], fr.at[r ^ 1], 0, 1)

    for r in (3, 2, 0, 1):
        send(piece(0, r), piece(2, r ^ 2), xs.at[r], xr.at[r ^ 2], 0, 2)
    send_on_z(0)
    for r in (1,):
        send(piece(0, r), piece(1, r ^ 1), ss.at[r], sr.at[r ^ 1], 0, 1)
    arrived(piece(1, 0), sr.at[0])
    send_on_z(1)
    fetch_residues.wait()

    def spread(r):
        start = pl.multiple_of(cols[r] * quarter, quarter)
        codes = residues[pl.ds(start, quarter), :]
        for symbol in range(SYMBOLS):
            onehot[symbol, r * quarter : (r + 1) * quarter, :] = jnp.where(
                codes == symbol, 1.0, 0.0
            ).astype(jnp.bfloat16)

    def agreement(r):
        products = jnp.dot(left[...], gathered[r], preferred_element_type=jnp.float32)
        return sigmoid_of(products, feature_length)

    spread(0)
    pass_to_sibling(1)
    pass_to_sibling(0)
    for r in (0, 3, 2):
        send(piece(0, r), piece(1, r ^ 1), ss.at[r], sr.at[r ^ 1], 0, 1)
    send_on_z(2)
    arrived(piece(3, 0), fr.at[0])
    send_on_z(3)
    sums = []
    for r in range(COLS):
        if r > 0:
            spread(r)
        if r > 1:
            pass_to_sibling(r)
        if r == 1 or r == 3:
            for q in (r - 1, r):
                if q > 0:
                    arrived(piece(1, q), sr.at[q])
                    arrived(piece(3, q), fr.at[q])
                else:
                    left[...] = gathered[0].T
                sums.append(jnp.sum(agreement(q), axis=0, keepdims=True))

    for i, d in enumerate(distances):
        for slot in range(COLS):
            arrived(zone.at[i, pl.ds(slot * width, width), :], zr.at[i, slot])
        left[...] = zone[i].T
        across = jnp.zeros((quarter, 128), jnp.float32)
        for r in range(COLS):
            values = agreement(r)
            sums[r] = sums[r] + jnp.sum(values, axis=0, keepdims=True)
            for lane in range(0, quarter, 128):
                across = across + values[:, lane : lane + 128]
        back = jnp.sum(across.T, axis=0, keepdims=True)
        back_out[i] = jnp.broadcast_to(back, (8, quarter))
        for k in range(COLS):
            send(back_out.at[i], back_in.at[i, k], ks.at[i, k], kr.at[i, k], -d, k)
    for r in range(COLS):
        rows_out[r : r + 1, :] = sums[r]
        rows_out[r + COLS : r + COLS + 1, :] = sums[r]
    for k in range(1, COLS):
        send(rows_out, rows_in.at[k], cs.at[k], cr.at[k], 0, k)
    for k in range(1, COLS):
        arrived(rows_in.at[k], cr.at[k])
    for i in range(len(distances)):
        for k in range(COLS):
            arrived(back_in.at[i, k], kr.at[i, k])

    weights = []
    for r in range(COLS):
        terms = [sums[r]] + [rows_in[k, r ^ k : (r ^ k) + 1, :] for k in range(1, COLS)]
        counts = (terms[0] + terms[1]) + (terms[2] + terms[3])
        for i in range(len(distances)):
            counts = counts + back_in[i, r, 0:1, :]
        weights.append(1.0 / counts)
    local_total = jnp.sum(
        (weights[0] + weights[1]) + (weights[2] + weights[3]), axis=1, keepdims=True
    )

    whole = jnp.concatenate(weights, axis=1)
    high = whole.astype(jnp.bfloat16).astype(jnp.float32)
    rest = whole - high
    middle = rest.astype(jnp.bfloat16).astype(jnp.float32)
    low = rest - middle
    row = lax.broadcasted_iota(jnp.int32, (16, whole.shape[1]), 0)
    split = jnp.where(
        row == 0, high, jnp.where(row == 1, middle, jnp.where(row == 2, low, 0.0))
    ).astype(jnp.bfloat16)
    table_out[SYMBOLS:TABLE_ROWS, :] = jnp.broadcast_to(
        local_total, (TABLE_ROWS - SYMBOLS, table_out.shape[1])
    )
    offsets = sorted(range(1, n), key=lambda o: -min(o, n - o))
    for part in range(TABLE_ROWS // 8):
        for symbol in range(8 * part, min(8 * part + 8, SYMBOLS)):
            product = jnp.dot(split, onehot[symbol], preferred_element_type=jnp.float32)
            table_out[symbol : symbol + 1, :] = jnp.sum(product, axis=0, keepdims=True)
        for o in offsets:
            send(
                table_out.at[pl.ds(8 * part, 8), :], table_in.at[o, pl.ds(8 * part, 8), :],
                ps.at[o, part], pr.at[o, part], o, 0,
            )
    for part in range(TABLE_ROWS // 8):
        for o in range(1, n):
            arrived(table_in.at[o, pl.ds(8 * part, 8), :], pr.at[o, part])
    table = butterfly_sum([table_out[...]] + [table_in[o] for o in range(1, n)])
    weight_sum = table[SYMBOLS : SYMBOLS + 1, :]
    profile_ref[...] = table[:SYMBOLS, :] / weight_sum
    scale = (n * COLS * quarter) / weight_sum
    for r in range(COLS):
        scaled = weights[r] * scale
        for part in range(quarter // 128):
            weight_ref[pl.ds(cols[r] * (quarter // 128) + part, 1), :] = scaled[
                :, part * 128 : part * 128 + 128
            ]
    for copy in started:
        copy.wait_send()


def hand_over(weight_ref, profile_ref, weight_out, profile_out):
    weight_out[...] = weight_ref[...]
    profile_out[...] = profile_ref[...]


def body(n, embeddings, residues):
    rows, width = embeddings.shape
    columns = residues.shape[1]
    quarter = rows // COLS
    distances = round_distances(n)
    nd = len(distances)
    dma = pltpu.SemaphoreType.DMA
    weights, profile = pl.pallas_call(
        functools.partial(kernel, n, distances, quarter),
        out_shape=(
            jax.ShapeDtypeStruct((rows // 128, 128), jnp.float32),
            jax.ShapeDtypeStruct((SYMBOLS, columns), jnp.float32),
        ),
        in_specs=[pl.BlockSpec(memory_space=pltpu.HBM)] * 2,
        out_specs=[pl.BlockSpec(memory_space=pltpu.VMEM)] * 2,
        scratch_shapes=[
            pltpu.VMEM((COLS, width * COLS, quarter), jnp.bfloat16),
            pltpu.VMEM((nd, width * COLS, quarter), jnp.bfloat16),
            pltpu.VMEM((quarter, width * COLS), jnp.bfloat16),
            pltpu.VMEM((rows, columns), jnp.int32),
            pltpu.VMEM((SYMBOLS, rows, columns), jnp.bfloat16),
            pltpu.VMEM((8, quarter), jnp.float32),
            pltpu.VMEM((COLS, 8, quarter), jnp.float32),
            pltpu.VMEM((nd, 8, quarter), jnp.float32),
            pltpu.VMEM((nd, COLS, 8, quarter), jnp.float32),
            pltpu.VMEM((TABLE_ROWS, columns), jnp.float32),
            pltpu.VMEM((n, TABLE_ROWS, columns), jnp.float32),
            dma((COLS,)), dma,
            dma((COLS,)), dma((COLS,)), dma((COLS,)), dma((COLS,)), dma((COLS,)), dma((COLS,)),
            dma((nd, COLS)), dma((nd, COLS)), dma((COLS,)), dma((COLS,)),
            dma((nd, COLS)), dma((nd, COLS)), dma((n, TABLE_ROWS // 8)), dma((n, TABLE_ROWS // 8)),
        ],
        compiler_params=pltpu.CompilerParams(
            collective_id=0, has_side_effects=True, vmem_limit_bytes=62 * 1024 * 1024
        ),
    )(embeddings.T, residues)
    weights, profile = pl.pallas_call(
        hand_over,
        out_shape=(
            jax.ShapeDtypeStruct(weights.shape, jnp.float32),
            jax.ShapeDtypeStruct(profile.shape, jnp.float32),
        ),
    )(weights, profile)
    return weights.reshape(rows), profile


def solution(mesh):
    return jax.shard_map(
        functools.partial(body, mesh.shape["seq"]),
        mesh=mesh,
        in_specs=(P(("groups", "seq"), "col"), P(("groups", "seq"), "col")),
        out_specs=(P(("groups", "seq")), P(None, ("groups", "col"))),
        check_vma=False,
    )
```

```python
import functools
import math

import jax
import jax.numpy as jnp
from jax import lax
from jax.experimental import pallas as pl
from jax.experimental.pallas import tpu as pltpu
from jax.sharding import PartitionSpec as P

SYMBOLS = 21
TABLE_ROWS = 24
COLS = 4

similarity_limit = 0.5
sigmoid_sharpness_scale = 0.05


def round_distances(block_count):
    round_count = min(4, (block_count - 1) // 2)
    stride = max(1, block_count // 8)
    return [1 + r * stride for r in range(round_count)]


def butterfly_sum(terms):
    while len(terms) > 1:
        half = len(terms) // 2
        terms = [terms[i] + terms[i + half] for i in range(half)]
    return terms[0]


def sigmoid_of(products, feature_length):
    log2e = math.log2(math.e)
    slope = -log2e / (feature_length * sigmoid_sharpness_scale)
    shift = log2e * similarity_limit / sigmoid_sharpness_scale
    return 1.0 / (1.0 + jnp.exp2(jnp.minimum(products * slope + shift, 126.0)))


def kernel(
    n, distances, quarter,
    x_ref, res_ref, weight_ref, profile_ref,
    gathered, zone, left, residues, onehot, rows_out, rows_in, back_out, back_in, table_out, table_in,
    ls, rs, xs, xr, ss, sr, fs, fr, zs, zr, cs, cr, ks, kr, ps, pr,
):
    width = x_ref.shape[0]
    feature_length = width * COLS
    me = lax.axis_index("col")
    block = lax.axis_index("seq")
    group = lax.axis_index("groups")
    cols = [me, me + 1 - 2 * (me % 2), (me + 2) % 4, 3 - me]

    def device(o, k):
        return (group, lax.rem(block + (o % n), n), cols[k])

    def piece(slot, r):
        return gathered.at[r, pl.ds(slot * width, width), :]

    peers = {(0, k) for k in range(1, COLS)}
    peers |= {(s * d % n, k) for d in distances for s in (1, -1) for k in range(COLS)}
    peers |= {(o, 0) for o in range(1, n)}
    peers = sorted(peers)

    barrier = pltpu.get_barrier_semaphore()
    for o, k in peers:
        pl.semaphore_signal(
            barrier, inc=1, device_id=device(o, k), device_id_type=pl.DeviceIdType.MESH
        )
    loads = []
    for r in (3, 2, 0, 1):
        start = pl.multiple_of(cols[r] * quarter, quarter)
        loads.append(
            pltpu.make_async_copy(x_ref.at[:, pl.ds(start, quarter)], piece(0, r), ls.at[r])
        )
    fetch_residues = pltpu.make_async_copy(res_ref, residues, rs)
    for load in loads:
        load.start()
    fetch_residues.start()
    for load in loads:
        load.wait()
    pl.semaphore_wait(barrier, len(peers))

    started = []

    def send(src, dst, send_sem, recv_sem, o, k):
        copy = pltpu.make_async_remote_copy(
            src_ref=src, dst_ref=dst, send_sem=send_sem, recv_sem=recv_sem,
            device_id=device(o, k), device_id_type=pl.DeviceIdType.MESH,
        )
        copy.start()
        started.append(copy)

    def arrived(dst, recv_sem):
        pltpu.make_async_copy(dst, dst, recv_sem).wait()

    def send_on_z(slot):
        for i, d in enumerate(distances):
            send(
                piece(slot, 0), zone.at[i, pl.ds(slot * width, width), :],
                zs.at[i, slot], zr.at[i, slot], d, 0,
            )

    def pass_to_sibling(r):
        arrived(piece(2, r), xr.at[r])
        send(piece(2, r), piece(3, r ^ 1), fs.at[r], fr.at[r ^ 1], 0, 1)

    for r in (3, 2, 0, 1):
        send(piece(0, r), piece(2, r ^ 2), xs.at[r], xr.at[r ^ 2], 0, 2)
    send_on_z(0)
    for r in (1,):
        send(piece(0, r), piece(1, r ^ 1), ss.at[r], sr.at[r ^ 1], 0, 1)
    arrived(piece(1, 0), sr.at[0])
    send_on_z(1)
    fetch_residues.wait()

    def spread(r):
        start = pl.multiple_of(cols[r] * quarter, quarter)
        codes = residues[pl.ds(start, quarter), :]
        for symbol in range(SYMBOLS):
            onehot[symbol, r * quarter : (r + 1) * quarter, :] = jnp.where(
                codes == symbol, 1.0, 0.0
            ).astype(jnp.bfloat16)

    def agreement(which, r):
        products = jnp.dot(left[which], gathered[r], preferred_element_type=jnp.float32)
        return sigmoid_of(products, feature_length)

    spread(0)
    pass_to_sibling(1)
    arrived(piece(3, 0), fr.at[0])
    send_on_z(3)
    pass_to_sibling(0)
    send_on_z(2)
    for r in (0, 3, 2):
        send(piece(0, r), piece(1, r ^ 1), ss.at[r], sr.at[r ^ 1], 0, 1)
    sums = []

    def add_own(r):
        if r > 0:
            arrived(piece(1, r), sr.at[r])
            arrived(piece(3, r), fr.at[r])
        else:
            left[0] = gathered[0].T
        sums.append(jnp.sum(agreement(0, r), axis=0, keepdims=True))

    spread(1)
    add_own(0)
    add_own(1)
    spread(2)
    pass_to_sibling(2)
    spread(3)
    pass_to_sibling(3)
    add_own(2)
    if not distances:
        add_own(3)

    for i, d in enumerate(distances):
        for slot in range(COLS):
            arrived(zone.at[i, pl.ds(slot * width, width), :], zr.at[i, slot])
        left[1] = zone[i].T
        across = jnp.zeros((quarter, 128), jnp.float32)
        for r in range(COLS):
            if r == len(sums):
                add_own(r)
            values = agreement(1, r)
            sums[r] = sums[r] + jnp.sum(values, axis=0, keepdims=True)
            for lane in range(0, quarter, 128):
                across = across + values[:, lane : lane + 128]
        back = jnp.sum(across.T, axis=0, keepdims=True)
        back_out[i] = jnp.broadcast_to(back, (8, quarter))
        for k in range(COLS):
            send(back_out.at[i], back_in.at[i, k], ks.at[i, k], kr.at[i, k], -d, k)
    for r in range(COLS):
        rows_out[r : r + 1, :] = sums[r]
        rows_out[r + COLS : r + COLS + 1, :] = sums[r]
    for k in range(1, COLS):
        send(rows_out, rows_in.at[k], cs.at[k], cr.at[k], 0, k)
    for k in range(1, COLS):
        arrived(rows_in.at[k], cr.at[k])
    for i in range(len(distances)):
        for k in range(COLS):
            arrived(back_in.at[i, k], kr.at[i, k])

    weights = []
    for r in range(COLS):
        terms = [sums[r]] + [rows_in[k, r ^ k : (r ^ k) + 1, :] for k in range(1, COLS)]
        counts = (terms[0] + terms[1]) + (terms[2] + terms[3])
        for i in range(len(distances)):
            counts = counts + back_in[i, r, 0:1, :]
        weights.append(1.0 / counts)
    local_total = jnp.sum(
        (weights[0] + weights[1]) + (weights[2] + weights[3]), axis=1, keepdims=True
    )

    whole = jnp.concatenate(weights, axis=1)
    high = whole.astype(jnp.bfloat16).astype(jnp.float32)
    rest = whole - high
    middle = rest.astype(jnp.bfloat16).astype(jnp.float32)
    low = rest - middle
    row = lax.broadcasted_iota(jnp.int32, (16, whole.shape[1]), 0)
    split = jnp.where(
        row == 0, high, jnp.where(row == 1, middle, jnp.where(row == 2, low, 0.0))
    ).astype(jnp.bfloat16)
    table_out[SYMBOLS:TABLE_ROWS, :] = jnp.broadcast_to(
        local_total, (TABLE_ROWS - SYMBOLS, table_out.shape[1])
    )
    offsets = sorted(range(1, n), key=lambda o: -min(o, n - o))
    for part in range(TABLE_ROWS // 8):
        for symbol in range(8 * part, min(8 * part + 8, SYMBOLS)):
            product = jnp.dot(split, onehot[symbol], preferred_element_type=jnp.float32)
            table_out[symbol : symbol + 1, :] = jnp.sum(product, axis=0, keepdims=True)
        for o in offsets:
            send(
                table_out.at[pl.ds(8 * part, 8), :], table_in.at[o, pl.ds(8 * part, 8), :],
                ps.at[o, part], pr.at[o, part], o, 0,
            )
    for part in range(TABLE_ROWS // 8):
        for o in range(1, n):
            arrived(table_in.at[o, pl.ds(8 * part, 8), :], pr.at[o, part])
    table = butterfly_sum([table_out[...]] + [table_in[o] for o in range(1, n)])
    weight_sum = table[SYMBOLS : SYMBOLS + 1, :]
    profile_ref[...] = table[:SYMBOLS, :] / weight_sum
    scale = (n * COLS * quarter) / weight_sum
    for r in range(COLS):
        scaled = weights[r] * scale
        for part in range(quarter // 128):
            weight_ref[pl.ds(cols[r] * (quarter // 128) + part, 1), :] = scaled[
                :, part * 128 : part * 128 + 128
            ]
    for copy in started:
        copy.wait_send()


def hand_over(weight_ref, profile_ref, weight_out, profile_out):
    weight_out[...] = weight_ref[...]
    profile_out[...] = profile_ref[...]


def body(n, embeddings, residues):
    rows, width = embeddings.shape
    columns = residues.shape[1]
    quarter = rows // COLS
    distances = round_distances(n)
    nd = len(distances)
    dma = pltpu.SemaphoreType.DMA
    weights, profile = pl.pallas_call(
        functools.partial(kernel, n, distances, quarter),
        out_shape=(
            jax.ShapeDtypeStruct((rows // 128, 128), jnp.float32),
            jax.ShapeDtypeStruct((SYMBOLS, columns), jnp.float32),
        ),
        in_specs=[pl.BlockSpec(memory_space=pltpu.HBM)] * 2,
        out_specs=[pl.BlockSpec(memory_space=pltpu.VMEM)] * 2,
        scratch_shapes=[
            pltpu.VMEM((COLS, width * COLS, quarter), jnp.bfloat16),
            pltpu.VMEM((nd, width * COLS, quarter), jnp.bfloat16),
            pltpu.VMEM((2, quarter, width * COLS), jnp.bfloat16),
            pltpu.VMEM((rows, columns), jnp.int32),
            pltpu.VMEM((SYMBOLS, rows, columns), jnp.bfloat16),
            pltpu.VMEM((8, quarter), jnp.float32),
            pltpu.VMEM((COLS, 8, quarter), jnp.float32),
            pltpu.VMEM((nd, 8, quarter), jnp.float32),
            pltpu.VMEM((nd, COLS, 8, quarter), jnp.float32),
            pltpu.VMEM((TABLE_ROWS, columns), jnp.float32),
            pltpu.VMEM((n, TABLE_ROWS, columns), jnp.float32),
            dma((COLS,)), dma,
            dma((COLS,)), dma((COLS,)), dma((COLS,)), dma((COLS,)), dma((COLS,)), dma((COLS,)),
            dma((nd, COLS)), dma((nd, COLS)), dma((COLS,)), dma((COLS,)),
            dma((nd, COLS)), dma((nd, COLS)), dma((n, TABLE_ROWS // 8)), dma((n, TABLE_ROWS // 8)),
        ],
        compiler_params=pltpu.CompilerParams(
            collective_id=0, has_side_effects=True, vmem_limit_bytes=62 * 1024 * 1024
        ),
    )(embeddings.T, residues)
    weights, profile = pl.pallas_call(
        hand_over,
        out_shape=(
            jax.ShapeDtypeStruct(weights.shape, jnp.float32),
            jax.ShapeDtypeStruct(profile.shape, jnp.float32),
        ),
    )(weights, profile)
    return weights.reshape(rows), profile


def solution(mesh):
    return jax.shard_map(
        functools.partial(body, mesh.shape["seq"]),
        mesh=mesh,
        in_specs=(P(("groups", "seq"), "col"), P(("groups", "seq"), "col")),
        out_specs=(P(("groups", "seq")), P(None, ("groups", "col"))),
        check_vma=False,
    )
```
